32 devices in a mesh: dp: 8 (over y, x, core), seq: 4 (over z).
Axes of the slice: x: 2, y: 2, z: 4, core: 2. Of those that a mesh axis runs over, the one named last changes fastest.
Arguments:
- patches: bfloat16 [12288, 128], P(('dp', 'seq')), parts along dimension 0, as said below
- pos_embed: bfloat16 [1536, 1024], P('seq'), may hold values from -3 to 3
- w_in: bfloat16 [128, 1024], replicated, may hold values from -0.5 to 0.5
- b_in: float32 [1024], replicated, may hold values from -3 to 3
- ln_gain: float32 [1024], replicated, may hold values from 0.5 to 1.5
- w_query: bfloat16 [1024, 1024], replicated, as said below
- w_key: bfloat16 [1024, 1024], replicated, as said below
- w_value: bfloat16 [1024, 1024], replicated, may hold values from -0.1875 to 0.1875
- w_proj: bfloat16 [1024, 1024], replicated, may hold values from -0.75 to 0.75
- out_gain: float32 [1024], replicated, may hold values from 0.5 to 1.5
- w_out: bfloat16 [1024, 256], replicated, may hold values from -0.09375 to 0.09375
- b_out: float32 [256], replicated, may hold values from -2 to 2
Outputs:
- latent: float32 [12288, 128], P(('dp', 'seq')), parts along dimension 0
- logdet: float32 [12288], P(('dp', 'seq')), parts along dimension 0
The draws below stay inside these ranges and needn't reach their ends.
There are 8 independent parts, one for each index of `dp`. The reference program is written for one: setup_inputs(seed, part) draws one part's arguments, and reference() takes and returns one part's arrays. A program takes and returns all parts, laid end to end along the dimension named above; an argument that names none is the same for every part. Nothing has to cross between parts.
Inputs may be any that keep to these rules, and one draw needn't show every extreme that they name: real-valued patches. `w_query`: real-valued query weights. `w_key`: real-valued key weights.
All inputs are finite; a program needn't handle non-finite values.
Results may differ from the reference program's by a relative error of at most 0.0084.
Values may be sent and summed in bfloat16 or wider, within the bound.
No kernel may reach another device: no remote copies, remote signals or barrier semaphores. Data moves between devices by JAX's collectives and lax.ppermute only.
A program may use at most 128 MiB of HBM per device.

```python
import math
import jax
import jax.numpy as jnp
from jax import lax

D = 1024
H = 8
HD = 128
P_SIZE = 128
S = 1536


def draw_patches(key, part):
    base = jax.random.normal(jax.random.fold_in(key, 21), (S, P_SIZE), jnp.float32)
    return base.astype(jnp.bfloat16)


def attention_pair(key):
    first = jax.random.normal(jax.random.fold_in(key, 31), (D, D), jnp.float32) * (2.0 / math.sqrt(D))
    second = jax.random.normal(jax.random.fold_in(key, 32), (D, D), jnp.float32) * (1.0 / math.sqrt(D))
    return (first, second)


def draw_w_query(key, part):
    first, second = attention_pair(key)
    return first.astype(jnp.bfloat16)


def draw_w_key(key, part):
    first, second = attention_pair(key)
    return second.astype(jnp.bfloat16)


def block_levels(rng, extent, shards, low, top_value):
    level = 1.0
    for dim, parts in shards:
        draws = jax.random.uniform(jax.random.fold_in(jax.random.fold_in(rng, 6), dim), (parts,), jnp.float32, low / len(shards), top_value / len(shards))
        level = level * jnp.repeat(jnp.exp(draws), extent[dim] // parts).reshape((-1,) + (1,) * (len(extent) - 1 - dim))
    return level


def normal_values(key, dims, width, limit, cuts=(), kind=jnp.bfloat16):
    level = block_levels(key, dims, cuts, -0.22, 0.18) if cuts else 1.0
    drawn = jax.random.normal(key, dims, jnp.float32) * width * level
    return jnp.minimum(jnp.maximum(drawn, -limit), limit).astype(kind)


def setup_inputs(seed: int = 0, part: int = 0) -> dict:
    streams_of = jax.random.split(jax.random.key(seed), 13)
    own_keys = jax.random.split(jax.random.fold_in(streams_of[12], part), 13)
    return {
        "patches": draw_patches(jax.random.fold_in(jax.random.fold_in(streams_of[12], part), 71), part),
        "pos_embed": normal_values(streams_of[1], (S, D), 0.5, 3.0, ((0, 4),)),
        "w_in": normal_values(streams_of[2], (P_SIZE, D), P_SIZE ** -0.5, 0.5),
        "b_in": normal_values(streams_of[3], (D,), 0.5, 3.0, (), jnp.float32),
        "ln_gain": jnp.clip(jax.random.uniform(streams_of[4], (D,), jnp.float32, 0.5, 1.5), 0.5, 1.5),
        "w_query": draw_w_query(jax.random.fold_in(streams_of[12], 71), part),
        "w_key": draw_w_key(jax.random.fold_in(streams_of[12], 71), part),
        "w_value": normal_values(streams_of[7], (D, D), D ** -0.5, 0.1875),
        "w_proj": normal_values(streams_of[8], (D, D), (D // 16) ** -0.5, 0.75),
        "out_gain": jnp.clip(jax.random.uniform(streams_of[9], (D,), jnp.float32, 0.5, 1.5), 0.5, 1.5),
        "w_out": normal_values(streams_of[10], (D, 2 * P_SIZE), (4 * D) ** -0.5, 0.09375),
        "b_out": normal_values(streams_of[11], (2 * P_SIZE,), 0.3, 2.0, (), jnp.float32),
    }


def normalize(values, gain):
    mean = lax.optimization_barrier(jnp.mean(values, axis=-1, keepdims=True))
    centred = values - mean
    spread = lax.optimization_barrier(jnp.mean(centred * centred, axis=-1, keepdims=True))
    return centred * lax.rsqrt(spread + 1e-05) * gain

def reference(patches, pos_embed, w_in, b_in, ln_gain, w_query, w_key, w_value, w_proj, out_gain, w_out, b_out):
    flipped = patches[::-1]
    shifted = jnp.concatenate([jnp.zeros((1, P_SIZE), patches.dtype), flipped[:-1]], axis=0)
    hidden = jnp.dot(shifted, w_in, preferred_element_type=jnp.float32) + b_in + pos_embed.astype(jnp.float32)
    normed = normalize(hidden, ln_gain).astype(jnp.bfloat16)
    queries = jnp.dot(normed, w_query, preferred_element_type=jnp.float32).astype(jnp.bfloat16)
    keys = jnp.dot(normed, w_key, preferred_element_type=jnp.float32).astype(jnp.bfloat16)
    values = jnp.dot(normed, w_value, preferred_element_type=jnp.float32).astype(jnp.bfloat16)
    scale = 1.0 / math.sqrt(HD)
    position = jnp.arange(S, dtype=jnp.int32)
    allowed = position[None, :] <= position[:, None]

    def head_out(head):
        start = (head * HD).astype(jnp.int32)
        query_head = lax.dynamic_slice_in_dim(queries, start, HD, 1)
        key_head = lax.dynamic_slice_in_dim(keys, start, HD, 1)
        value_head = lax.dynamic_slice_in_dim(values, start, HD, 1)
        scores = jnp.dot(query_head, key_head.T, preferred_element_type=jnp.float32) * scale
        scores = jnp.where(allowed, scores, -1e+30)
        top = lax.optimization_barrier(jnp.max(scores, axis=1, keepdims=True))
        weights = jnp.where(allowed, jnp.exp(scores - top), 0.0)
        total = lax.optimization_barrier(jnp.sum(weights, axis=1, keepdims=True))
        return jnp.dot(weights.astype(jnp.bfloat16), value_head, preferred_element_type=jnp.float32) / total
    heads = lax.map(head_out, jnp.arange(H, dtype=jnp.int32))
    attended = jnp.transpose(heads, (1, 0, 2)).reshape(S, D).astype(jnp.bfloat16)
    mixed = hidden + jnp.dot(attended, w_proj, preferred_element_type=jnp.float32)
    second = normalize(mixed, out_gain).astype(jnp.bfloat16)
    stats = jnp.dot(second, w_out, preferred_element_type=jnp.float32) + b_out
    shift_part = stats[:, :P_SIZE]
    log_scale = stats[:, P_SIZE:]
    latent = (flipped.astype(jnp.float32) - shift_part) * jnp.exp(-log_scale)
    logdet = -lax.optimization_barrier(jnp.mean(log_scale, axis=1))
    return (latent, logdet)
```

```python
import functools
import math

import jax
import jax.numpy as jnp
from jax import lax
from jax.experimental import pallas as pl
from jax.experimental.pallas import tpu as pltpu
from jax.sharding import PartitionSpec as P

H = 8
LANES = 128
PAD = 16
F32 = jnp.float32
BF16 = jnp.bfloat16
VMEM = pltpu.VMEM


def dot(a, b):
    return jnp.dot(a, b, preferred_element_type=F32)


def normalize(values, gain):
    mean = jnp.mean(values, axis=-1, keepdims=True)
    centred = values - mean
    spread = jnp.mean(centred * centred, axis=-1, keepdims=True)
    return centred * lax.rsqrt(spread + 1e-05) * gain


def place_patches(slots, refs, held, rows, me):
    if slots is None:
        held[: held.shape[0] - PAD] = refs[0][...]
    else:
        for slot, ref in zip(slots, refs):
            start = pl.multiple_of(jnp.bitwise_xor(me, slot) * rows, rows)
            held[pl.ds(start, rows)] = ref[...]
    held[held.shape[0] - PAD :] = jnp.zeros((PAD, held.shape[1]), BF16)


def window(held, block, rows, count):
    start = pl.multiple_of((count - 1 - block) * rows, rows)
    return held[pl.ds(start, rows + PAD)]


def reverse(part, last):
    rows = part.shape[0] - PAD
    row = lax.broadcasted_iota(jnp.int32, (rows, rows + PAD), 0)
    col = lax.broadcasted_iota(jnp.int32, (rows, rows + PAD), 1)
    return dot((row + col == last).astype(BF16), part)


def hidden_of(part, pos, w_in, b_in):
    rows = part.shape[0] - PAD
    shifted = reverse(part, rows).astype(BF16)
    return dot(shifted, w_in) + b_in + pos.astype(F32)


def scores_of(queries, keys):
    return lax.dot_general(queries, keys, (((1,), (1,)), ((), ())), preferred_element_type=F32)


def repeat(column, width):
    return jnp.concatenate([column] * (width // LANES), axis=1)


def with_ones(values):
    return jnp.concatenate([values, jnp.ones((values.shape[0], LANES), BF16)], axis=1)


def own_kernel(
    slots, count, n_patch, *refs
):
    patch_refs = refs[:n_patch]
    (pos, w_in, b_in, gain, w_query, w_key, w_value) = refs[n_patch : n_patch + 7]
    (hidden_out, query_out, acc_out, top_out, held) = refs[n_patch + 7 :]
    rows = pos.shape[0]
    head = w_query.shape[1] // H
    me = lax.axis_index("seq")
    place_patches(slots, patch_refs, held, rows, me)
    hidden = hidden_of(window(held, me, rows, count), pos[...], w_in[...], b_in[...])
    hidden_out[...] = hidden
    normed = normalize(hidden, gain[...]).astype(BF16)
    scale = math.log2(math.e) / math.sqrt(head)
    query_out[...] = (dot(normed, w_query[...]) * scale).astype(BF16)
    keys = dot(normed, w_key[...]).astype(BF16)
    values = dot(normed, w_value[...]).astype(BF16)
    row = lax.broadcasted_iota(jnp.int32, (rows, rows), 0)
    col = lax.broadcasted_iota(jnp.int32, (rows, rows), 1)
    allowed = col <= row
    for h in range(H):
        part = slice(h * head, (h + 1) * head)
        scores = jnp.where(allowed, scores_of(query_out[:, part], keys[:, part]), -1e30)
        top = jnp.broadcast_to(jnp.max(scores, axis=1, keepdims=True), (rows, LANES))
        weights = jnp.exp2(scores - repeat(top, rows)).astype(BF16)
        top_out[h] = top
        acc_out[h] = dot(weights, with_ones(values[:, part]))


def rest_kernel(slots, count, n_patch, n_pos, *refs):
    patch_refs = refs[:n_patch]
    pos_refs = refs[n_patch : n_patch + n_pos]
    (hidden, query, acc_in, top_in, w_in, b_in, gain, w_key, w_value, w_proj, out_gain, w_out, b_out) = refs[
        n_patch + n_pos : n_patch + n_pos + 13
    ]
    (latent_out, logdet_out, held, pos_held, acc, top) = refs[n_patch + n_pos + 13 :]
    rows, width = hidden.shape
    head = width // H
    feats = patch_refs[0].shape[1]
    me = lax.axis_index("seq")
    place_patches(slots, patch_refs, held, rows, me)
    acc[...] = acc_in[...]
    top[...] = top_in[...]
    if slots is not None:
        group = lax.axis_index("dp")
        for piece, ref in enumerate(pos_refs):
            pos_held[jnp.bitwise_xor(group, piece)] = ref[...]

    def add_block(block, pos):
        hid = hidden_of(window(held, block, rows, count), pos, w_in[...], b_in[...])
        normed = normalize(hid, gain[...]).astype(BF16)
        keys = dot(normed, w_key[...]).astype(BF16)
        values = dot(normed, w_value[...]).astype(BF16)
        for h in range(H):
            part = slice(h * head, (h + 1) * head)
            scores = scores_of(query[:, part], keys[:, part])
            old = top[h]
            new = jnp.maximum(old, jnp.max(scores, axis=1, keepdims=True))
            weights = jnp.exp2(scores - repeat(new, rows)).astype(BF16)
            factor = jnp.exp2(old - new)
            top[h] = new
            acc[h] = acc[h] * repeat(factor, head + LANES) + dot(weights, with_ones(values[:, part]))

    if slots is None:

        def step(block, carry):
            add_block(block, pos_refs[0][block])
            return carry

        lax.fori_loop(0, me, step, 0)
    else:
        for place in range(count - 1):
            block = jnp.bitwise_xor(me, place + 1)

            @pl.when(block < me)
            def _():
                chunks = [pos_held[c, place * rows : (place + 1) * rows] for c in range(pos_held.shape[0])]
                add_block(block, jnp.concatenate(chunks, axis=1))

    attended = jnp.concatenate([(acc[h][:, :head] / acc[h][:, head:]).astype(BF16) for h in range(H)], axis=1)
    mixed = hidden[...] + dot(attended, w_proj[...])
    second = normalize(mixed, out_gain[...]).astype(BF16)
    stats = dot(second, w_out[...]) + b_out[...]
    shift_part = stats[:, :feats]
    log_scale = stats[:, feats:]
    flipped = reverse(window(held, me, rows, count), rows - 1)
    latent_out[...] = (flipped - shift_part) * jnp.exp(-log_scale)
    logdet_out[...] = -jnp.mean(jnp.transpose(log_scale), axis=0, keepdims=True)


def spec(n):
    return [pl.BlockSpec(memory_space=VMEM)] * n


def shards(
    patches, pos_embed, w_in, b_in, ln_gain, w_query, w_key, w_value, w_proj, out_gain, w_out, b_out
):
    count = lax.axis_size("seq")
    groups = lax.axis_size("dp")
    rows, feats = patches.shape
    width = w_query.shape[0]
    head = width // H
    b_in, ln_gain, out_gain, b_out = [a.reshape(1, -1) for a in (b_in, ln_gain, out_gain, b_out)]
    quick = count == 4 and groups == 8 and width == groups * LANES
    if quick:
        group = lax.axis_index("dp")
        cut = lax.dynamic_slice_in_dim(pos_embed, group * LANES, LANES, 1)

        def swap(block, axis, mask, size):
            return lax.ppermute(block, axis, [(i, i ^ mask) for i in range(size)])

        along = [swap(cut, "seq", m, count) for m in (1, 2, 3)]
        slots = (0, 1, 2, 3)
        patch_list = [patches] + [swap(patches, "seq", m, count) for m in (1, 2, 3)]
        mine = jnp.concatenate(along, axis=0)
        plane = [mine] + [swap(mine, "dp", m, groups) for m in (2, 4, 6)]
        other = [swap(block, "dp", 1, groups) for block in plane]
        pos_list = []
        for a, b in zip(plane, other):
            pos_list += [a, b]
        own_slots = (0, 2, 3)
        own_patches = [patch_list[s] for s in own_slots]
    else:
        slots = own_slots = None
        patch_list = own_patches = [lax.all_gather(patches, "seq", axis=0, tiled=True)]
        pos_list = [lax.all_gather(pos_embed, "seq", axis=0, tiled=False)]
    held = VMEM((count * rows + PAD, feats), BF16)
    own = pl.pallas_call(
        functools.partial(own_kernel, own_slots, count, len(own_patches)),
        out_shape=(
            jax.ShapeDtypeStruct((rows, width), F32),
            jax.ShapeDtypeStruct((rows, width), BF16),
            jax.ShapeDtypeStruct((H, rows, head + LANES), F32),
            jax.ShapeDtypeStruct((H, rows, LANES), F32),
        ),
        in_specs=spec(len(own_patches) + 7),
        out_specs=spec(4),
        scratch_shapes=[held],
        compiler_params=pltpu.CompilerParams(vmem_limit_bytes=24 << 20),
        cost_estimate=pl.CostEstimate(flops=6 << 30, bytes_accessed=12 << 20, transcendentals=0),
        name="own_block",
    )(*own_patches, pos_embed, w_in, b_in, ln_gain, w_query, w_key, w_value)
    hidden, query, acc, top = own
    pos_shape = (groups, (count - 1) * rows, LANES) if quick else (8, LANES)
    latent, logdet = pl.pallas_call(
        functools.partial(rest_kernel, slots, count, len(patch_list), len(pos_list)),
        out_shape=(
            jax.ShapeDtypeStruct((rows, feats), F32),
            jax.ShapeDtypeStruct((1, rows), F32),
        ),
        in_specs=spec(len(patch_list) + len(pos_list) + 13),
        out_specs=spec(2),
        scratch_shapes=[
            held,
            VMEM(pos_shape, BF16),
            VMEM((H, rows, head + LANES), F32),
            VMEM((H, rows, LANES), F32),
        ],
        compiler_params=pltpu.CompilerParams(vmem_limit_bytes=24 << 20),
        cost_estimate=pl.CostEstimate(flops=12 << 30, bytes_accessed=16 << 20, transcendentals=0),
        name="rest_blocks",
    )(*patch_list, *pos_list, hidden, query, acc, top, w_in, b_in, ln_gain, w_key, w_value, w_proj, out_gain, w_out, b_out)
    return (latent, logdet.reshape(rows))


def solution(mesh):
    in_specs = (
        P(("dp", "seq"), None),
        P("seq", None),
        P(),
        P(),
        P(),
        P(),
        P(),
        P(),
        P(),
        P(),
        P(),
        P(),
    )
    out_specs = (P(("dp", "seq"), None), P(("dp", "seq")))
    return jax.shard_map(shards, mesh=mesh, in_specs=in_specs, out_specs=out_specs, check_vma=False)
```

```python
import functools
import math

import jax
import jax.numpy as jnp
from jax import lax
from jax.experimental import pallas as pl
from jax.experimental.pallas import tpu as pltpu
from jax.sharding import PartitionSpec as P

H = 8
LANES = 128
PAD = 16
F32 = jnp.float32
BF16 = jnp.bfloat16
VMEM = pltpu.VMEM
HBM = pltpu.HBM


def dot(a, b):
    return jnp.dot(a, b, preferred_element_type=F32)


def normalize(values, gain):
    mean = jnp.mean(values, axis=-1, keepdims=True)
    centred = values - mean
    spread = jnp.mean(centred * centred, axis=-1, keepdims=True)
    return centred * lax.rsqrt(spread + 1e-05) * gain


def place_patches(slots, refs, held, rows, me):
    if slots is None:
        held[: held.shape[0] - PAD] = refs[0][...]
    else:
        for slot, ref in zip(slots, refs):
            start = pl.multiple_of(jnp.bitwise_xor(me, slot) * rows, rows)
            held[pl.ds(start, rows)] = ref[...]
    held[held.shape[0] - PAD :] = jnp.zeros((PAD, held.shape[1]), BF16)


def window(held, block, rows, count):
    start = pl.multiple_of((count - 1 - block) * rows, rows)
    return held[pl.ds(start, rows + PAD)]


def reverse(part, last):
    rows = part.shape[0] - PAD
    row = lax.broadcasted_iota(jnp.int32, (rows, rows + PAD), 0)
    col = lax.broadcasted_iota(jnp.int32, (rows, rows + PAD), 1)
    return dot((row + col == last).astype(BF16), part)


def from_patches(part, w_in, b_in):
    rows = part.shape[0] - PAD
    return dot(reverse(part, rows).astype(BF16), w_in) + b_in


def scores_of(queries, keys):
    return lax.dot_general(queries, keys, (((1,), (1,)), ((), ())), preferred_element_type=F32)


def repeat(column, width):
    return jnp.concatenate([column] * (width // LANES), axis=1)


def with_ones(values):
    return jnp.concatenate([values, jnp.ones((values.shape[0], LANES), BF16)], axis=1)


def load_kernel(n, *refs):
    sems = refs[2 * n]
    moves = [pltpu.make_async_copy(refs[i], refs[n + i], sems.at[i]) for i in range(n)]
    for move in moves:
        move.start()
    for move in moves:
        move.wait()


def own_kernel(slots, places, count, n_patch, *refs):
    patch_refs = refs[:n_patch]
    (pos, w_in, b_in, gain, w_query, w_key, w_value) = refs[n_patch : n_patch + 7]
    (hidden_out, query_out, acc_out, top_out, parts_out, flipped_out, held) = refs[n_patch + 7 :]
    rows = pos.shape[0]
    head = w_query.shape[1] // H
    me = lax.axis_index("seq")
    place_patches(slots, patch_refs, held, rows, me)
    own = window(held, me, rows, count)
    flipped_out[...] = reverse(own, rows - 1)
    hidden = from_patches(own, w_in[...], b_in[...]) + pos[...].astype(F32)
    hidden_out[...] = hidden
    normed = normalize(hidden, gain[...]).astype(BF16)
    scale = math.log2(math.e) / math.sqrt(head)
    query_out[...] = (dot(normed, w_query[...]) * scale).astype(BF16)
    keys = dot(normed, w_key[...]).astype(BF16)
    values = dot(normed, w_value[...]).astype(BF16)
    row = lax.broadcasted_iota(jnp.int32, (rows, rows), 0)
    col = lax.broadcasted_iota(jnp.int32, (rows, rows), 1)
    allowed = col <= row
    ahead = scores_of(query_out[:, :head], keys[:, :head])
    for h in range(H):
        scores = jnp.where(allowed, ahead, -1e30)
        if h + 1 < H:
            part = slice((h + 1) * head, (h + 2) * head)
            ahead = scores_of(query_out[:, part], keys[:, part])
        top = jnp.broadcast_to(jnp.max(scores, axis=1, keepdims=True), (rows, LANES))
        weights = jnp.exp2(scores - repeat(top, rows)).astype(BF16)
        top_out[h] = top
        acc_out[h] = dot(weights, with_ones(values[:, h * head : (h + 1) * head]))
    if slots is None:

        def step(block, carry):
            parts_out[block] = from_patches(window(held, block, rows, count), w_in[...], b_in[...])
            return carry

        lax.fori_loop(0, me, step, 0)
    else:
        for i, place in enumerate(places):
            block = jnp.bitwise_xor(me, place)
            parts_out[i] = from_patches(window(held, block, rows, count), w_in[...], b_in[...])


def add_block(query, hid, gain, w_key, w_value, acc, top, bias):
    rows = query.shape[0]
    head = query.shape[1] // H
    normed = normalize(hid, gain[...]).astype(BF16)
    keys = dot(normed, w_key[...]).astype(BF16)
    values = dot(normed, w_value[...]).astype(BF16)
    ahead = scores_of(query[:, :head], keys[:, :head])
    for h in range(H):
        scores = ahead
        if h + 1 < H:
            part = slice((h + 1) * head, (h + 2) * head)
            ahead = scores_of(query[:, part], keys[:, part])
        old = top[h]
        new = jnp.maximum(old, jnp.max(scores, axis=1, keepdims=True) - bias)
        weights = jnp.exp2(scores - repeat(new + bias, rows)).astype(BF16)
        factor = jnp.exp2(old - new)
        top[h] = new
        acc[h] = acc[h] * repeat(factor, head + LANES) + dot(weights, with_ones(values[:, h * head : (h + 1) * head]))


def place_positions(mine, other, pos_held):
    group = lax.axis_index("dp")
    for i in range(mine.shape[0]):
        pos_held[jnp.bitwise_xor(group, 2 * i)] = mine[i]
        pos_held[jnp.bitwise_xor(group, 2 * i + 1)] = other[i]


def rest_kernel(places, n_pos, *refs):
    (hidden, query, _, _, parts, flipped) = refs[:6]
    pos_refs = refs[6 : n_pos + 6]
    weights = refs[n_pos + 6 : n_pos + 9]
    (w_proj, out_gain, w_out, b_out) = refs[n_pos + 9 : n_pos + 13]
    (latent_out, logdet_out, acc, top) = refs[n_pos + 13 : n_pos + 17]
    rows, width = hidden.shape
    head = width // H
    feats = flipped.shape[1]
    me = lax.axis_index("seq")
    if places is None:

        def step(block, carry):
            add_block(query, parts[block] + pos_refs[0][block].astype(F32), *weights, acc, top, 0.0)
            return carry

        lax.fori_loop(0, me, step, 0)
    else:
        pos_held = refs[-1]
        place_positions(*pos_refs, pos_held)
        for i, place in enumerate(places):
            bias = jnp.where(jnp.bitwise_xor(me, place) < me, 0.0, 1e30).astype(F32)
            pos = [pos_held[c, i * rows : (i + 1) * rows] for c in range(pos_held.shape[0])]
            hid = parts[i] + jnp.concatenate(pos, axis=1).astype(F32)
            add_block(query, hid, *weights, acc, top, bias)
    attended = jnp.concatenate([(acc[h][:, :head] / acc[h][:, head:]).astype(BF16) for h in range(H)], axis=1)
    mixed = hidden[...] + dot(attended, w_proj[...])
    second = normalize(mixed, out_gain[...]).astype(BF16)
    stats = dot(second, w_out[...]) + b_out[...]
    shift_part = stats[:, :feats]
    log_scale = stats[:, feats:]
    latent_out[...] = (flipped[...] - shift_part) * jnp.exp(-log_scale)
    logdet_out[...] = -jnp.mean(jnp.transpose(log_scale), axis=0)


def spec(n, memory=VMEM):
    return [pl.BlockSpec(memory_space=memory)] * n


def stay(array):
    return pltpu.with_memory_space_constraint(array, HBM)


def cost(flops):
    return pl.CostEstimate(flops=flops, bytes_accessed=1 << 20, transcendentals=0)


def shards(
    patches, pos_embed, w_in, b_in, ln_gain, w_query, w_key, w_value, w_proj, out_gain, w_out, b_out
):
    count = lax.axis_size("seq")
    groups = lax.axis_size("dp")
    rows, feats = patches.shape
    width = w_query.shape[0]
    head = width // H
    b_in, ln_gain, out_gain, b_out = [a.reshape(1, -1) for a in (b_in, ln_gain, out_gain, b_out)]
    quick = count == 4 and groups == 8 and width == groups * LANES
    if quick:
        group = lax.axis_index("dp")
        cut = lax.dynamic_slice_in_dim(pos_embed, group * LANES, LANES, 1)

        def swap(block, axis, mask, size):
            return lax.ppermute(block, axis, [(i, i ^ mask) for i in range(size)])

        def send(block, pairs):
            return lax.ppermute(block, "seq", pairs)

        along = [
            send(cut, [(2, 3), (0, 1)]),
            send(cut, [(1, 3), (0, 2)]),
            send(cut, [(0, 3), (1, 2)]),
        ]
        after = lax.optimization_barrier((patches, cut))[0]
        patch_list = [
            patches,
            send(after, [(2, 3), (3, 2)]),
            send(after, [(1, 3), (3, 1)]),
            send(after, [(0, 3), (1, 2), (2, 1), (3, 0)]),
        ]
        slots = (0, 1, 2, 3)
        places = (1, 2, 3)
    else:
        slots = places = None
        patch_list = [lax.all_gather(patches, "seq", axis=0, tiled=True)]
        pos_list = [lax.all_gather(pos_embed, "seq", axis=0, tiled=False)]
    own_given = (pos_embed, w_in, b_in, ln_gain, w_query, w_key, w_value)
    if quick:
        own_given = pl.pallas_call(
            functools.partial(load_kernel, len(own_given)),
            out_shape=[VMEM(a.shape, a.dtype) for a in own_given],
            in_specs=spec(len(own_given), HBM),
            out_specs=spec(len(own_given)),
            scratch_shapes=[pltpu.SemaphoreType.DMA((len(own_given),))],
            compiler_params=pltpu.CompilerParams(vmem_limit_bytes=1 << 20),
            cost_estimate=cost(1),
            name="load_weights",
        )(*[stay(a) for a in own_given])
        own_given = list(own_given)
        *along, own_given[1] = lax.optimization_barrier((*along, own_given[1]))
        *patch_list[1:], own_given[1] = lax.optimization_barrier((*patch_list[1:], own_given[1]))
        mine = jnp.concatenate(along, axis=0)
        plane = [mine] + [swap(mine, "dp", m, groups) for m in (2, 4, 6)]
    (_, w_in, b_in, ln_gain, _, w_key, w_value) = own_given
    state = (
        jax.ShapeDtypeStruct((H, rows, head + LANES), F32),
        jax.ShapeDtypeStruct((H, rows, LANES), F32),
    )
    n = len(patch_list)
    hidden, query, acc, top, parts, flipped = pl.pallas_call(
        functools.partial(own_kernel, slots, places, count, n),
        out_shape=(
            jax.ShapeDtypeStruct((rows, width), F32),
            jax.ShapeDtypeStruct((rows, width), BF16),
            *state,
            jax.ShapeDtypeStruct((count - 1, rows, width), F32),
            jax.ShapeDtypeStruct((rows, feats), F32),
        ),
        in_specs=spec(n + 7),
        out_specs=spec(6),
        scratch_shapes=[VMEM((count * rows + PAD, feats), BF16)],
        compiler_params=pltpu.CompilerParams(vmem_limit_bytes=(16 if quick else 52) << 20),
        cost_estimate=cost(1),
        name="own_block",
    )(*patch_list, *own_given)
    if quick:
        query, *plane = lax.optimization_barrier((query, *plane))
        plane = jnp.stack(plane)
        pos_list = (plane, swap(plane, "dp", 1, groups))
    n = len(pos_list)
    latent, logdet, _, _ = pl.pallas_call(
        functools.partial(rest_kernel, places, n),
        out_shape=(jax.ShapeDtypeStruct((rows, feats), F32), jax.ShapeDtypeStruct((rows,), F32)) + state,
        in_specs=spec(n + 13),
        out_specs=spec(4),
        scratch_shapes=[VMEM((groups, (count - 1) * rows, LANES), BF16)] if quick else [],
        input_output_aliases={2: 2, 3: 3},
        compiler_params=pltpu.CompilerParams(vmem_limit_bytes=(20 if quick else 60) << 20),
        cost_estimate=cost(1),
        name="other_blocks",
    )(hidden, query, acc, top, parts, flipped, *pos_list, ln_gain, w_key, w_value, w_proj, out_gain, w_out, b_out)
    return (latent, logdet)


def solution(mesh):
    in_specs = (
        P(("dp", "seq"), None),
        P("seq", None),
        P(),
        P(),
        P(),
        P(),
        P(),
        P(),
        P(),
        P(),
        P(),
        P(),
    )
    out_specs = (P(("dp", "seq"), None), P(("dp", "seq")))
    return jax.shard_map(shards, mesh=mesh, in_specs=in_specs, out_specs=out_specs, check_vma=False)
```

```python
import functools
import math

import jax
import jax.numpy as jnp
from jax import lax
from jax.experimental import pallas as pl
from jax.experimental.pallas import tpu as pltpu
from jax.sharding import PartitionSpec as P

H = 8
LANES = 128
PAD = 16
F32 = jnp.float32
BF16 = jnp.bfloat16
VMEM = pltpu.VMEM
HBM = pltpu.HBM


def dot(a, b):
    return jnp.dot(a, b, preferred_element_type=F32)


def normalize(values, gain):
    mean = jnp.mean(values, axis=-1, keepdims=True)
    centred = values - mean
    spread = jnp.mean(centred * centred, axis=-1, keepdims=True)
    return centred * lax.rsqrt(spread + 1e-05) * gain


def place_patches(slots, refs, held, rows, me):
    if slots is None:
        held[: held.shape[0] - PAD] = refs[0][...]
    else:
        for slot, ref in zip(slots, refs):
            start = pl.multiple_of(jnp.bitwise_xor(me, slot) * rows, rows)
            held[pl.ds(start, rows)] = ref[...]
    held[held.shape[0] - PAD :] = jnp.zeros((PAD, held.shape[1]), BF16)


def window(held, block, rows, count):
    start = pl.multiple_of((count - 1 - block) * rows, rows)
    return held[pl.ds(start, rows + PAD)]


def reverse(part, last):
    rows = part.shape[0] - PAD
    row = lax.broadcasted_iota(jnp.int32, (rows, rows + PAD), 0)
    col = lax.broadcasted_iota(jnp.int32, (rows, rows + PAD), 1)
    return dot((row + col == last).astype(BF16), part)


def from_patches(part, w_in, b_in):
    rows = part.shape[0] - PAD
    return dot(reverse(part, rows).astype(BF16), w_in) + b_in


def scores_of(queries, keys):
    return lax.dot_general(queries, keys, (((1,), (1,)), ((), ())), preferred_element_type=F32)


def repeat(column, width):
    return jnp.concatenate([column] * (width // LANES), axis=1)


def with_ones(values):
    return jnp.concatenate([values, jnp.ones((values.shape[0], LANES), BF16)], axis=1)


def load_kernel(n, *refs):
    sems = refs[2 * n]
    moves = [pltpu.make_async_copy(refs[i], refs[n + i], sems.at[i]) for i in range(n)]
    for move in moves:
        move.start()
    for move in moves:
        move.wait()


def own_kernel(slots, places, count, n_patch, *refs):
    patch_refs = refs[:n_patch]
    (w_in, b_in, pos, gain) = refs[n_patch : n_patch + 4]
    given = refs[n_patch + 4 : n_patch + 7]
    (hidden_out, query_out, acc_out, top_out, parts_out, flipped_out, w_key, w_value) = refs[n_patch + 7 : n_patch + 15]
    (held, w_query, sems) = refs[n_patch + 15 :]
    moves = [pltpu.make_async_copy(a, b, sems.at[i]) for i, (a, b) in enumerate(zip(given, (w_query, w_key, w_value)))]
    for move in moves:
        move.start()
    rows = pos.shape[0]
    head = w_query.shape[1] // H
    me = lax.axis_index("seq")
    place_patches(slots, patch_refs, held, rows, me)
    if slots is None:

        def step(block, carry):
            parts_out[block] = from_patches(window(held, block, rows, count), w_in[...], b_in[...])
            return carry

        lax.fori_loop(0, me, step, 0)
    else:
        for i, place in enumerate(places):
            block = jnp.bitwise_xor(me, place)
            parts_out[i] = from_patches(window(held, block, rows, count), w_in[...], b_in[...])
    own = window(held, me, rows, count)
    flipped_out[...] = reverse(own, rows - 1)
    hidden = from_patches(own, w_in[...], b_in[...]) + pos[...].astype(F32)
    hidden_out[...] = hidden
    normed = normalize(hidden, gain[...]).astype(BF16)
    scale = math.log2(math.e) / math.sqrt(head)
    moves[0].wait()
    query_out[...] = (dot(normed, w_query[...]) * scale).astype(BF16)
    moves[1].wait()
    keys = dot(normed, w_key[...]).astype(BF16)
    moves[2].wait()
    values = dot(normed, w_value[...]).astype(BF16)
    row = lax.broadcasted_iota(jnp.int32, (rows, rows), 0)
    col = lax.broadcasted_iota(jnp.int32, (rows, rows), 1)
    allowed = col <= row
    ahead = scores_of(query_out[:, :head], keys[:, :head])
    for h in range(H):
        scores = jnp.where(allowed, ahead, -1e30)
        if h + 1 < H:
            part = slice((h + 1) * head, (h + 2) * head)
            ahead = scores_of(query_out[:, part], keys[:, part])
        top = jnp.broadcast_to(jnp.max(scores, axis=1, keepdims=True), (rows, LANES))
        weights = jnp.exp2(scores - repeat(top, rows)).astype(BF16)
        top_out[h] = top
        acc_out[h] = dot(weights, with_ones(values[:, h * head : (h + 1) * head]))


def add_block(query, hid, gain, w_key, w_value, acc, top):
    rows = query.shape[0]
    head = query.shape[1] // H
    normed = normalize(hid, gain[...]).astype(BF16)
    keys = dot(normed, w_key[...]).astype(BF16)
    values = dot(normed, w_value[...]).astype(BF16)
    for h in range(H):
        part = slice(h * head, (h + 1) * head)
        scores = scores_of(query[:, part], keys[:, part])
        old = top[h]
        new = jnp.maximum(old, jnp.max(scores, axis=1, keepdims=True))
        weights = jnp.exp2(scores - repeat(new, rows)).astype(BF16)
        factor = jnp.exp2(old - new)
        top[h] = new
        acc[h] = acc[h] * repeat(factor, head + LANES) + dot(weights, with_ones(values[:, part]))


def add_blocks(query, places, parts, pos_held, gain, w_key, w_value, normed, keys, values, acc, top):
    rows = query.shape[0]
    head = query.shape[1] // H
    me = lax.axis_index("seq")
    biases, spans = [], []
    for i, place in enumerate(places):
        biases.append(jnp.where(jnp.bitwise_xor(me, place) < me, 0.0, 1e30).astype(F32))
        span = slice(i * rows, (i + 1) * rows)
        spans.append(span)
        pos = jnp.concatenate([pos_held[c, span] for c in range(pos_held.shape[0])], axis=1)
        normed[span] = normalize(parts[i] + pos.astype(F32), gain[...]).astype(BF16)
        keys[span] = dot(normed[span], w_key[...]).astype(BF16)
        values[span] = dot(normed[span], w_value[...]).astype(BF16)
    ahead = scores_of(query[:, :head], keys[:, :head])
    for h in range(H):
        scores = ahead
        if h + 1 < H:
            part = slice((h + 1) * head, (h + 2) * head)
            ahead = scores_of(query[:, part], keys[:, part])
        old = new = top[h]
        for span, bias in zip(spans, biases):
            new = jnp.maximum(new, jnp.max(scores[:, span], axis=1, keepdims=True) - bias)
        pieces = [jnp.exp2(scores[:, span] - repeat(new + bias, rows)).astype(BF16) for span, bias in zip(spans, biases)]
        factor = jnp.exp2(old - new)
        weights = jnp.concatenate(pieces, axis=1)
        acc[h] = acc[h] * repeat(factor, head + LANES) + dot(weights, with_ones(values[:, h * head : (h + 1) * head]))


def place_positions(mine, other, pos_held):
    group = lax.axis_index("dp")
    for i in range(mine.shape[0]):
        pos_held[jnp.bitwise_xor(group, 2 * i)] = mine[i]
        pos_held[jnp.bitwise_xor(group, 2 * i + 1)] = other[i]


def rest_kernel(places, n_pos, *refs):
    (hidden, query, _, _, parts, flipped) = refs[:6]
    pos_refs = refs[6 : n_pos + 6]
    weights = refs[n_pos + 6 : n_pos + 9]
    (w_proj, out_gain, w_out, b_out) = refs[n_pos + 9 : n_pos + 13]
    (latent_out, logdet_out, acc, top) = refs[n_pos + 13 : n_pos + 17]
    rows, width = hidden.shape
    head = width // H
    feats = flipped.shape[1]
    me = lax.axis_index("seq")
    if places is None:

        def step(block, carry):
            add_block(query, parts[block] + pos_refs[0][block].astype(F32), *weights, acc, top)
            return carry

        lax.fori_loop(0, me, step, 0)
    else:
        (pos_held, normed, keys, values) = refs[n_pos + 17 :]
        place_positions(*pos_refs, pos_held)
        add_blocks(query, places, parts, pos_held, *weights, normed, keys, values, acc, top)
    attended = jnp.concatenate([(acc[h][:, :head] / acc[h][:, head:]).astype(BF16) for h in range(H)], axis=1)
    mixed = hidden[...] + dot(attended, w_proj[...])
    second = normalize(mixed, out_gain[...]).astype(BF16)
    stats = dot(second, w_out[...]) + b_out[...]
    shift_part = stats[:, :feats]
    log_scale = stats[:, feats:]
    latent_out[...] = (flipped[...] - shift_part) * jnp.exp(-log_scale)
    logdet_out[...] = -jnp.mean(jnp.transpose(log_scale), axis=0)


def spec(n, memory=VMEM):
    return [pl.BlockSpec(memory_space=memory)] * n


def stay(array):
    return pltpu.with_memory_space_constraint(array, HBM)


def cost(flops):
    return pl.CostEstimate(flops=flops, bytes_accessed=1 << 20, transcendentals=0)


def shards(
    patches, pos_embed, w_in, b_in, ln_gain, w_query, w_key, w_value, w_proj, out_gain, w_out, b_out
):
    count = lax.axis_size("seq")
    groups = lax.axis_size("dp")
    rows, feats = patches.shape
    width = w_query.shape[0]
    head = width // H
    b_in, ln_gain, out_gain, b_out = [a.reshape(1, -1) for a in (b_in, ln_gain, out_gain, b_out)]
    quick = count == 4 and groups == 8 and width == groups * LANES
    if quick:
        group = lax.axis_index("dp")
        cut = lax.dynamic_slice_in_dim(pos_embed, group * LANES, LANES, 1)

        def swap(block, axis, mask, size):
            return lax.ppermute(block, axis, [(i, i ^ mask) for i in range(size)])

        def send(block, pairs):
            return lax.ppermute(block, "seq", pairs)

        along = [
            send(cut, [(2, 3), (0, 1)]),
            send(cut, [(1, 3), (0, 2)]),
            send(cut, [(0, 3), (1, 2)]),
        ]
        after = lax.optimization_barrier((patches, cut))[0]
        patch_list = [
            patches,
            send(after, [(2, 3), (3, 2)]),
            send(after, [(1, 3), (3, 1)]),
            send(after, [(0, 3), (1, 2), (2, 1), (3, 0)]),
        ]
        slots = (0, 1, 2, 3)
        places = (1, 2, 3)
    else:
        slots = places = None
        patch_list = [lax.all_gather(patches, "seq", axis=0, tiled=True)]
        pos_list = [lax.all_gather(pos_embed, "seq", axis=0, tiled=False)]
    own_given = (w_in, b_in, pos_embed, ln_gain)
    if quick:
        own_given = pl.pallas_call(
            functools.partial(load_kernel, len(own_given)),
            out_shape=[VMEM(a.shape, a.dtype) for a in own_given],
            in_specs=spec(len(own_given), HBM),
            out_specs=spec(len(own_given)),
            scratch_shapes=[pltpu.SemaphoreType.DMA((len(own_given),))],
            compiler_params=pltpu.CompilerParams(vmem_limit_bytes=1 << 20),
            cost_estimate=cost(1),
            name="load_weights",
        )(*[stay(a) for a in own_given])
        own_given = list(own_given)
        *along, own_given[1] = lax.optimization_barrier((*along, own_given[1]))
        *patch_list[1:], own_given[1] = lax.optimization_barrier((*patch_list[1:], own_given[1]))
        mine = jnp.concatenate(along, axis=0)
        plane = [mine] + [swap(mine, "dp", m, groups) for m in (2, 4, 6)]
        ln_gain = own_given[3]
    here = VMEM if quick else jax.ShapeDtypeStruct
    state = (here((H, rows, head + LANES), F32), here((H, rows, LANES), F32))
    n = len(patch_list)
    hidden, query, acc, top, parts, flipped, w_key, w_value = pl.pallas_call(
        functools.partial(own_kernel, slots, places, count, n),
        out_shape=(
            here((rows, width), F32),
            here((rows, width), BF16),
            *state,
            here((count - 1, rows, width), F32),
            here((rows, feats), F32),
            here(w_key.shape, BF16),
            here(w_value.shape, BF16),
        ),
        in_specs=spec(n + 4) + spec(3, HBM),
        out_specs=spec(8),
        scratch_shapes=[
            VMEM((count * rows + PAD, feats), BF16),
            VMEM(w_query.shape, BF16),
            pltpu.SemaphoreType.DMA((3,)),
        ],
        compiler_params=pltpu.CompilerParams(vmem_limit_bytes=(20 if quick else 54) << 20),
        cost_estimate=cost(1 << 36),
        name="own_block",
    )(*patch_list, *own_given, *[stay(a) for a in (w_query, w_key, w_value)])
    if quick:
        query, *plane = lax.optimization_barrier((query, *plane))
        plane = jnp.stack(plane)
        pos_list = (plane, swap(plane, "dp", 1, groups))
    n = len(pos_list)
    latent, logdet, _, _ = pl.pallas_call(
        functools.partial(rest_kernel, places, n),
        out_shape=(jax.ShapeDtypeStruct((rows, feats), F32), jax.ShapeDtypeStruct((rows,), F32)) + state,
        in_specs=spec(n + 13),
        out_specs=spec(4),
        scratch_shapes=[VMEM((groups, (count - 1) * rows, LANES), BF16)] + [VMEM(((count - 1) * rows, width), BF16)] * 3
        if quick
        else [],
        input_output_aliases={2: 2, 3: 3},
        compiler_params=pltpu.CompilerParams(vmem_limit_bytes=(20 if quick else 60) << 20),
        cost_estimate=cost(1),
        name="other_blocks",
    )(hidden, query, acc, top, parts, flipped, *pos_list, ln_gain, w_key, w_value, w_proj, out_gain, w_out, b_out)
    return (latent, logdet)


def solution(mesh):
    in_specs = (
        P(("dp", "seq"), None),
        P("seq", None),
        P(),
        P(),
        P(),
        P(),
        P(),
        P(),
        P(),
        P(),
        P(),
        P(),
    )
    out_specs = (P(("dp", "seq"), None), P(("dp", "seq")))
    return jax.shard_map(shards, mesh=mesh, in_specs=in_specs, out_specs=out_specs, check_vma=False)
```

```python
import functools
import math

import jax
import jax.numpy as jnp
from jax import lax
from jax.experimental import pallas as pl
from jax.experimental.pallas import tpu as pltpu
from jax.sharding import PartitionSpec as P

H = 8
LANES = 128
PAD = 16
F32 = jnp.float32
BF16 = jnp.bfloat16
VMEM = pltpu.VMEM
HBM = pltpu.HBM


def dot(a, b):
    return jnp.dot(a, b, preferred_element_type=F32)


def normalize(values, gain):
    mean = jnp.mean(values, axis=-1, keepdims=True)
    centred = values - mean
    spread = jnp.mean(centred * centred, axis=-1, keepdims=True)
    return centred * lax.rsqrt(spread + 1e-05) * gain


def place_patches(slots, refs, held, rows, me):
    if slots is None:
        held[: held.shape[0] - PAD] = refs[0][...]
    else:
        for slot, ref in zip(slots, refs):
            start = pl.multiple_of(jnp.bitwise_xor(me, slot) * rows, rows)
            held[pl.ds(start, rows)] = ref[...]
    held[held.shape[0] - PAD :] = jnp.zeros((PAD, held.shape[1]), BF16)


def window(held, block, rows, count):
    start = pl.multiple_of((count - 1 - block) * rows, rows)
    return held[pl.ds(start, rows + PAD)]


def reverse(part, last):
    rows = part.shape[0] - PAD
    row = lax.broadcasted_iota(jnp.int32, (rows, rows + PAD), 0)
    col = lax.broadcasted_iota(jnp.int32, (rows, rows + PAD), 1)
    return dot((row + col == last).astype(BF16), part)


def from_patches(part, w_in, b_in):
    rows = part.shape[0] - PAD
    return dot(reverse(part, rows).astype(BF16), w_in) + b_in


def scores_of(queries, keys):
    return lax.dot_general(queries, keys, (((1,), (1,)), ((), ())), preferred_element_type=F32)


def repeat(column, width):
    return jnp.concatenate([column] * (width // LANES), axis=1)


def with_ones(values):
    return jnp.concatenate([values, jnp.ones((values.shape[0], LANES), BF16)], axis=1)


def first_kernel(*refs):
    given = refs[:5]
    (w_in, pos, gain, own, b_in, cut, sems) = refs[5:]
    moves = [pltpu.make_async_copy(a, b, sems.at[i]) for i, (a, b) in enumerate(zip(given, refs[5:10]))]
    for move in moves:
        move.start()
    for move in moves:
        move.wait()
    cut[...] = pos[:, pl.ds(pl.multiple_of(lax.axis_index("dp") * LANES, LANES), LANES)]


def parts_kernel(slots, places, count, n_patch, *refs):
    patch_refs = refs[:n_patch]
    (w_in, b_in, parts_out, held) = refs[n_patch:]
    rows = parts_out.shape[1]
    me = lax.axis_index("seq")
    place_patches(slots, patch_refs, held, rows, me)
    if slots is None:

        def step(block, carry):
            parts_out[block] = from_patches(window(held, block, rows, count), w_in[...], b_in[...])
            return carry

        lax.fori_loop(0, me, step, 0)
    else:
        for i, place in enumerate(places):
            block = jnp.bitwise_xor(me, place)
            parts_out[i] = from_patches(window(held, block, rows, count), w_in[...], b_in[...])


def own_kernel(slots, count, n_patch, *refs):
    patch_refs = refs[:n_patch]
    (w_in, b_in, pos, gain, w_query, w_key, w_value) = refs[n_patch : n_patch + 7]
    (hidden_out, query_out, acc_out, top_out, flipped_out, held) = refs[n_patch + 7 :]
    rows = pos.shape[0]
    head = w_query.shape[1] // H
    me = lax.axis_index("seq")
    place_patches(slots, patch_refs, held, rows, me)
    own = window(held, me, rows, count)
    flipped_out[...] = reverse(own, rows - 1)
    hidden = from_patches(own, w_in[...], b_in[...]) + pos[...].astype(F32)
    hidden_out[...] = hidden
    normed = normalize(hidden, gain[...]).astype(BF16)
    scale = math.log2(math.e) / math.sqrt(head)
    query_out[...] = (dot(normed, w_query[...]) * scale).astype(BF16)
    keys = dot(normed, w_key[...]).astype(BF16)
    values = dot(normed, w_value[...]).astype(BF16)
    row = lax.broadcasted_iota(jnp.int32, (rows, rows), 0)
    col = lax.broadcasted_iota(jnp.int32, (rows, rows), 1)
    allowed = col <= row
    ahead = scores_of(query_out[:, :head], keys[:, :head])
    for h in range(H):
        scores = jnp.where(allowed, ahead, -1e30)
        if h + 1 < H:
            part = slice((h + 1) * head, (h + 2) * head)
            ahead = scores_of(query_out[:, part], keys[:, part])
        top = jnp.broadcast_to(jnp.max(scores, axis=1, keepdims=True), (rows, LANES))
        weights = jnp.exp2(scores - repeat(top, rows)).astype(BF16)
        top_out[h] = top
        acc_out[h] = dot(weights, with_ones(values[:, h * head : (h + 1) * head]))


def add_block(query, hid, gain, w_key, w_value, acc, top):
    rows = query.shape[0]
    head = query.shape[1] // H
    normed = normalize(hid, gain[...]).astype(BF16)
    keys = dot(normed, w_key[...]).astype(BF16)
    values = dot(normed, w_value[...]).astype(BF16)
    for h in range(H):
        part = slice(h * head, (h + 1) * head)
        scores = scores_of(query[:, part], keys[:, part])
        old = top[h]
        new = jnp.maximum(old, jnp.max(scores, axis=1, keepdims=True))
        weights = jnp.exp2(scores - repeat(new, rows)).astype(BF16)
        factor = jnp.exp2(old - new)
        top[h] = new
        acc[h] = acc[h] * repeat(factor, head + LANES) + dot(weights, with_ones(values[:, part]))


def add_blocks(query, places, parts, pos_held, gain, w_key, w_value, normed, keys, values, acc, top):
    rows = query.shape[0]
    head = query.shape[1] // H
    me = lax.axis_index("seq")
    biases, spans = [], []
    for i, place in enumerate(places):
        biases.append(jnp.where(jnp.bitwise_xor(me, place) < me, 0.0, 1e30).astype(F32))
        span = slice(i * rows, (i + 1) * rows)
        spans.append(span)
        pos = jnp.concatenate([pos_held[c, span] for c in range(pos_held.shape[0])], axis=1)
        normed[span] = normalize(parts[i] + pos.astype(F32), gain[...]).astype(BF16)
        keys[span] = dot(normed[span], w_key[...]).astype(BF16)
        values[span] = dot(normed[span], w_value[...]).astype(BF16)
    ahead = scores_of(query[:, :head], keys[:, :head])
    for h in range(H):
        scores = ahead
        if h + 1 < H:
            part = slice((h + 1) * head, (h + 2) * head)
            ahead = scores_of(query[:, part], keys[:, part])
        old = new = top[h]
        for span, bias in zip(spans, biases):
            new = jnp.maximum(new, jnp.max(scores[:, span], axis=1, keepdims=True) - bias)
        pieces = [jnp.exp2(scores[:, span] - repeat(new + bias, rows)).astype(BF16) for span, bias in zip(spans, biases)]
        factor = jnp.exp2(old - new)
        weights = jnp.concatenate(pieces, axis=1)
        acc[h] = acc[h] * repeat(factor, head + LANES) + dot(weights, with_ones(values[:, h * head : (h + 1) * head]))


def place_positions(mine, other, pos_held):
    group = lax.axis_index("dp")
    for i in range(mine.shape[0]):
        pos_held[jnp.bitwise_xor(group, 2 * i)] = mine[i]
        pos_held[jnp.bitwise_xor(group, 2 * i + 1)] = other[i]


def rest_kernel(places, n_pos, *refs):
    (hidden, query, _, _, parts, flipped) = refs[:6]
    pos_refs = refs[6 : n_pos + 6]
    weights = refs[n_pos + 6 : n_pos + 9]
    (w_proj, out_gain, w_out, b_out) = refs[n_pos + 9 : n_pos + 13]
    (latent_out, logdet_out, acc, top) = refs[n_pos + 13 : n_pos + 17]
    rows, width = hidden.shape
    head = width // H
    feats = flipped.shape[1]
    me = lax.axis_index("seq")
    if places is None:

        def step(block, carry):
            add_block(query, parts[block] + pos_refs[0][block].astype(F32), *weights, acc, top)
            return carry

        lax.fori_loop(0, me, step, 0)
    else:
        (pos_held, normed, keys, values) = refs[n_pos + 17 :]
        place_positions(*pos_refs, pos_held)
        add_blocks(query, places, parts, pos_held, *weights, normed, keys, values, acc, top)
    attended = jnp.concatenate([(acc[h][:, :head] / acc[h][:, head:]).astype(BF16) for h in range(H)], axis=1)
    mixed = hidden[...] + dot(attended, w_proj[...])
    second = normalize(mixed, out_gain[...]).astype(BF16)
    stats = dot(second, w_out[...]) + b_out[...]
    shift_part = stats[:, :feats]
    log_scale = stats[:, feats:]
    latent_out[...] = (flipped[...] - shift_part) * jnp.exp(-log_scale)
    logdet_out[...] = -jnp.mean(jnp.transpose(log_scale), axis=0)


def spec(n, memory=VMEM):
    return [pl.BlockSpec(memory_space=memory)] * n


def stay(array):
    return pltpu.with_memory_space_constraint(array, HBM)


def cost(flops):
    return pl.CostEstimate(flops=flops, bytes_accessed=1 << 20, transcendentals=0)


def shards(
    patches, pos_embed, w_in, b_in, ln_gain, w_query, w_key, w_value, w_proj, out_gain, w_out, b_out
):
    count = lax.axis_size("seq")
    groups = lax.axis_size("dp")
    rows, feats = patches.shape
    width = w_query.shape[0]
    head = width // H
    b_in, ln_gain, out_gain, b_out = [a.reshape(1, -1) for a in (b_in, ln_gain, out_gain, b_out)]
    quick = count == 4 and groups == 8 and width == groups * LANES
    if quick:
        given = (w_in, pos_embed, ln_gain, patches, b_in)
        w_in, pos_embed, ln_gain, patches, b_in, cut = pl.pallas_call(
            first_kernel,
            out_shape=[VMEM(a.shape, a.dtype) for a in (*given, patches)],
            in_specs=spec(5, HBM),
            out_specs=spec(6),
            scratch_shapes=[pltpu.SemaphoreType.DMA((5,))],
            compiler_params=pltpu.CompilerParams(vmem_limit_bytes=1 << 20),
            cost_estimate=cost(1 << 34),
            name="first_loads",
        )(*[stay(a) for a in given])

        def swap(block, axis, mask, size):
            return lax.ppermute(block, axis, [(i, i ^ mask) for i in range(size)])

        def send(block, pairs):
            return lax.ppermute(block, "seq", pairs)

        places = (3, 1, 2)
        along = [
            send(cut, [(2, 3), (0, 1)]),
            send(cut, [(1, 3), (0, 2)]),
            send(cut, [(0, 3), (1, 2)]),
        ]
        mine = jnp.concatenate([along[m - 1] for m in places], axis=0)
        plane = [mine] + [swap(mine, "dp", m, groups) for m in (2, 4, 6)]
        later = lax.optimization_barrier((patches, mine))[0]
        patch_list = [
            patches,
            send(later, [(2, 3), (3, 2)]),
            send(patches, [(1, 3), (3, 1)]),
            send(patches, [(0, 3), (1, 2), (2, 1), (3, 0)]),
        ]
        slots = (0, 1, 2, 3)
        own_slots = (0, 2, 3)
        own_patches = [patch_list[i] for i in own_slots]
    else:
        slots = places = own_slots = None
        patch_list = own_patches = [lax.all_gather(patches, "seq", axis=0, tiled=True)]
        pos_list = [lax.all_gather(pos_embed, "seq", axis=0, tiled=False)]
    here = VMEM if quick else jax.ShapeDtypeStruct
    state = (here((H, rows, head + LANES), F32), here((H, rows, LANES), F32))
    held = VMEM((count * rows + PAD, feats), BF16)
    n = len(own_patches)
    hidden, query, acc, top, flipped = pl.pallas_call(
        functools.partial(own_kernel, own_slots, count, n),
        out_shape=(here((rows, width), F32), here((rows, width), BF16), *state, here((rows, feats), F32)),
        in_specs=spec(n + 7),
        out_specs=spec(5),
        scratch_shapes=[held],
        compiler_params=pltpu.CompilerParams(vmem_limit_bytes=(16 if quick else 48) << 20),
        cost_estimate=cost(1 << 36),
        name="own_block",
    )(*own_patches, w_in, b_in, pos_embed, ln_gain, w_query, w_key, w_value)
    n = len(patch_list)
    if quick:
        patch_list[1], query = lax.optimization_barrier((patch_list[1], query))
    parts = pl.pallas_call(
        functools.partial(parts_kernel, slots, places, count, n),
        out_shape=here((count - 1, rows, width), F32),
        in_specs=spec(n + 2),
        out_specs=spec(1)[0],
        scratch_shapes=[held],
        compiler_params=pltpu.CompilerParams(vmem_limit_bytes=(10 if quick else 48) << 20),
        cost_estimate=cost(1 << 30),
        name="patch_parts",
    )(*patch_list, w_in, b_in)
    if quick:
        parts, *plane = lax.optimization_barrier((parts, *plane))
        plane = jnp.stack(plane)
        pos_list = (plane, swap(plane, "dp", 1, groups))
    n = len(pos_list)
    latent, logdet, _, _ = pl.pallas_call(
        functools.partial(rest_kernel, places, n),
        out_shape=(jax.ShapeDtypeStruct((rows, feats), F32), jax.ShapeDtypeStruct((rows,), F32)) + state,
        in_specs=spec(n + 13),
        out_specs=spec(4),
        scratch_shapes=[VMEM((groups, (count - 1) * rows, LANES), BF16)] + [VMEM(((count - 1) * rows, width), BF16)] * 3
        if quick
        else [],
        input_output_aliases={2: 2, 3: 3},
        compiler_params=pltpu.CompilerParams(vmem_limit_bytes=(20 if quick else 60) << 20),
        cost_estimate=cost(1),
        name="other_blocks",
    )(hidden, query, acc, top, parts, flipped, *pos_list, ln_gain, w_key, w_value, w_proj, out_gain, w_out, b_out)
    return (latent, logdet)


def solution(mesh):
    in_specs = (
        P(("dp", "seq"), None),
        P("seq", None),
        P(),
        P(),
        P(),
        P(),
        P(),
        P(),
        P(),
        P(),
        P(),
        P(),
    )
    out_specs = (P(("dp", "seq"), None), P(("dp", "seq")))
    return jax.shard_map(shards, mesh=mesh, in_specs=in_specs, out_specs=out_specs, check_vma=False)
```

```python
import functools
import math

import jax
import jax.numpy as jnp
from jax import lax
from jax.experimental import pallas as pl
from jax.experimental.pallas import tpu as pltpu
from jax.sharding import PartitionSpec as P

H = 8
LANES = 128
PAD = 16
F32 = jnp.float32
BF16 = jnp.bfloat16
VMEM = pltpu.VMEM
HBM = pltpu.HBM


def dot(a, b):
    return jnp.dot(a, b, preferred_element_type=F32)


def normalize(values, gain):
    mean = jnp.mean(values, axis=-1, keepdims=True)
    centred = values - mean
    spread = jnp.mean(centred * centred, axis=-1, keepdims=True)
    return centred * lax.rsqrt(spread + 1e-05) * gain


def place_patches(slots, refs, held, rows, me):
    if slots is None:
        held[: held.shape[0] - PAD] = refs[0][...]
    else:
        for slot, ref in zip(slots, refs):
            start = pl.multiple_of(jnp.bitwise_xor(me, slot) * rows, rows)
            held[pl.ds(start, rows)] = ref[...]
    held[held.shape[0] - PAD :] = jnp.zeros((PAD, held.shape[1]), BF16)


def window(held, block, rows, count):
    start = pl.multiple_of((count - 1 - block) * rows, rows)
    return held[pl.ds(start, rows + PAD)]


def reverse(part, last):
    rows = part.shape[0] - PAD
    row = lax.broadcasted_iota(jnp.int32, (rows, rows + PAD), 0)
    col = lax.broadcasted_iota(jnp.int32, (rows, rows + PAD), 1)
    return dot((row + col == last).astype(BF16), part)


def from_patches(part, w_in, b_in):
    rows = part.shape[0] - PAD
    return dot(reverse(part, rows).astype(BF16), w_in) + b_in


def scores_of(queries, keys):
    return lax.dot_general(queries, keys, (((1,), (1,)), ((), ())), preferred_element_type=F32)


def repeat(column, width):
    return jnp.concatenate([column] * (width // LANES), axis=1)


def with_ones(values):
    return jnp.concatenate([values, jnp.ones((values.shape[0], LANES), BF16)], axis=1)


def first_kernel(*refs):
    given, pos, targets, sems = refs[:4], refs[4], refs[5:10], refs[10]
    columns = pl.ds(pl.multiple_of(lax.axis_index("dp") * LANES, LANES), LANES)
    sources = (*given, pos.at[:, columns])
    moves = [pltpu.make_async_copy(a, b, sems.at[i]) for i, (a, b) in enumerate(zip(sources, targets))]
    for move in moves:
        move.start()
    for move in moves:
        move.wait()


def parts_kernel(slots, places, count, n_patch, *refs):
    patch_refs = refs[:n_patch]
    (w_in, b_in, parts_out, held) = refs[n_patch:]
    rows = parts_out.shape[1]
    me = lax.axis_index("seq")
    place_patches(slots, patch_refs, held, rows, me)
    if slots is None:

        def step(block, carry):
            parts_out[block] = from_patches(window(held, block, rows, count), w_in[...], b_in[...])
            return carry

        lax.fori_loop(0, me, step, 0)
    else:
        for i, place in enumerate(places):
            block = jnp.bitwise_xor(me, place)
            parts_out[i] = from_patches(window(held, block, rows, count), w_in[...], b_in[...])


def own_kernel(slots, count, n_patch, *refs):
    patch_refs = refs[:n_patch]
    (w_in, b_in, pos, gain, w_query, w_key, w_value) = refs[n_patch : n_patch + 7]
    (hidden_out, query_out, acc_out, top_out, flipped_out, held) = refs[n_patch + 7 :]
    rows = pos.shape[0]
    head = w_query.shape[1] // H
    me = lax.axis_index("seq")
    place_patches(slots, patch_refs, held, rows, me)
    own = window(held, me, rows, count)
    flipped_out[...] = reverse(own, rows - 1)
    hidden = from_patches(own, w_in[...], b_in[...]) + pos[...].astype(F32)
    hidden_out[...] = hidden
    normed = normalize(hidden, gain[...]).astype(BF16)
    scale = math.log2(math.e) / math.sqrt(head)
    query_out[...] = (dot(normed, w_query[...]) * scale).astype(BF16)
    keys = dot(normed, w_key[...]).astype(BF16)
    values = dot(normed, w_value[...]).astype(BF16)
    row = lax.broadcasted_iota(jnp.int32, (rows, rows), 0)
    col = lax.broadcasted_iota(jnp.int32, (rows, rows), 1)
    allowed = col <= row
    ahead = scores_of(query_out[:, :head], keys[:, :head])
    for h in range(H):
        scores = jnp.where(allowed, ahead, -1e30)
        if h + 1 < H:
            part = slice((h + 1) * head, (h + 2) * head)
            ahead = scores_of(query_out[:, part], keys[:, part])
        top = jnp.broadcast_to(jnp.max(scores, axis=1, keepdims=True), (rows, LANES))
        weights = jnp.exp2(scores - repeat(top, rows)).astype(BF16)
        top_out[h] = top
        acc_out[h] = dot(weights, with_ones(values[:, h * head : (h + 1) * head]))


def add_block(query, hid, gain, w_key, w_value, acc, top):
    rows = query.shape[0]
    head = query.shape[1] // H
    normed = normalize(hid, gain[...]).astype(BF16)
    keys = dot(normed, w_key[...]).astype(BF16)
    values = dot(normed, w_value[...]).astype(BF16)
    for h in range(H):
        part = slice(h * head, (h + 1) * head)
        scores = scores_of(query[:, part], keys[:, part])
        old = top[h]
        new = jnp.maximum(old, jnp.max(scores, axis=1, keepdims=True))
        weights = jnp.exp2(scores - repeat(new, rows)).astype(BF16)
        factor = jnp.exp2(old - new)
        top[h] = new
        acc[h] = acc[h] * repeat(factor, head + LANES) + dot(weights, with_ones(values[:, part]))


def add_blocks(query, places, parts, pos_held, gain, w_key, w_value, normed, keys, values, acc, top):
    rows = query.shape[0]
    head = query.shape[1] // H
    me = lax.axis_index("seq")
    biases, spans = [], []
    for i, place in enumerate(places):
        biases.append(jnp.where(jnp.bitwise_xor(me, place) < me, 0.0, 1e30).astype(F32))
        span = slice(i * rows, (i + 1) * rows)
        spans.append(span)
        pos = jnp.concatenate([pos_held[c, span] for c in range(pos_held.shape[0])], axis=1)
        normed[span] = normalize(parts[i] + pos.astype(F32), gain[...]).astype(BF16)
        keys[span] = dot(normed[span], w_key[...]).astype(BF16)
        values[span] = dot(normed[span], w_value[...]).astype(BF16)
    ahead = scores_of(query[:, :head], keys[:, :head])
    for h in range(H):
        scores = ahead
        if h + 1 < H:
            part = slice((h + 1) * head, (h + 2) * head)
            ahead = scores_of(query[:, part], keys[:, part])
        old = new = top[h]
        for span, bias in zip(spans, biases):
            new = jnp.maximum(new, jnp.max(scores[:, span], axis=1, keepdims=True) - bias)
        pieces = [jnp.exp2(scores[:, span] - repeat(new + bias, rows)).astype(BF16) for span, bias in zip(spans, biases)]
        factor = jnp.exp2(old - new)
        weights = jnp.concatenate(pieces, axis=1)
        acc[h] = acc[h] * repeat(factor, head + LANES) + dot(weights, with_ones(values[:, h * head : (h + 1) * head]))


def place_positions(mine, near, plane, other, pos_held):
    group = lax.axis_index("dp")
    pos_held[group] = mine[...]
    pos_held[jnp.bitwise_xor(group, 1)] = near[...]
    for i in range(plane.shape[0]):
        pos_held[jnp.bitwise_xor(group, 2 * i + 2)] = plane[i]
        pos_held[jnp.bitwise_xor(group, 2 * i + 3)] = other[i]


def rest_kernel(places, n_pos, *refs):
    (hidden, query, _, _, parts, flipped) = refs[:6]
    pos_refs = refs[6 : n_pos + 6]
    weights = refs[n_pos + 6 : n_pos + 9]
    (w_proj, out_gain, w_out, b_out) = refs[n_pos + 9 : n_pos + 13]
    (latent_out, logdet_out, acc, top) = refs[n_pos + 13 : n_pos + 17]
    rows, width = hidden.shape
    head = width // H
    feats = flipped.shape[1]
    me = lax.axis_index("seq")
    if places is None:

        def step(block, carry):
            add_block(query, parts[block] + pos_refs[0][block].astype(F32), *weights, acc, top)
            return carry

        lax.fori_loop(0, me, step, 0)
    else:
        (pos_held, normed, keys, values) = refs[n_pos + 17 :]
        place_positions(*pos_refs, pos_held)
        add_blocks(query, places, parts, pos_held, *weights, normed, keys, values, acc, top)
    attended = jnp.concatenate([(acc[h][:, :head] / acc[h][:, head:]).astype(BF16) for h in range(H)], axis=1)
    mixed = hidden[...] + dot(attended, w_proj[...])
    second = normalize(mixed, out_gain[...]).astype(BF16)
    stats = dot(second, w_out[...]) + b_out[...]
    shift_part = stats[:, :feats]
    log_scale = stats[:, feats:]
    latent_out[...] = (flipped[...] - shift_part) * jnp.exp(-log_scale)
    logdet_out[...] = -jnp.mean(jnp.transpose(log_scale), axis=0)


def spec(n, memory=VMEM):
    return [pl.BlockSpec(memory_space=memory)] * n


def stay(array):
    return pltpu.with_memory_space_constraint(array, HBM)


def cost(flops):
    return pl.CostEstimate(flops=flops, bytes_accessed=1 << 20, transcendentals=0)


def shards(
    patches, pos_embed, w_in, b_in, ln_gain, w_query, w_key, w_value, w_proj, out_gain, w_out, b_out
):
    count = lax.axis_size("seq")
    groups = lax.axis_size("dp")
    rows, feats = patches.shape
    width = w_query.shape[0]
    head = width // H
    b_in, ln_gain, out_gain, b_out = [a.reshape(1, -1) for a in (b_in, ln_gain, out_gain, b_out)]
    quick = count == 4 and groups == 8 and width == groups * LANES
    if quick:
        given = (w_in, ln_gain, patches, b_in)
        w_in, ln_gain, patches, b_in, cut = pl.pallas_call(
            first_kernel,
            out_shape=[VMEM(a.shape, a.dtype) for a in (*given, patches)],
            in_specs=spec(5, HBM),
            out_specs=spec(5),
            scratch_shapes=[pltpu.SemaphoreType.DMA((5,))],
            compiler_params=pltpu.CompilerParams(vmem_limit_bytes=1 << 20),
            cost_estimate=cost(1 << 34),
            name="first_loads",
        )(*[stay(a) for a in (*given, pos_embed)])

        def swap(block, axis, mask, size):
            return lax.ppermute(block, axis, [(i, i ^ mask) for i in range(size)])

        def send(block, pairs):
            return lax.ppermute(block, "seq", pairs)

        places = (3, 1, 2)
        along = [
            send(cut, [(2, 3), (0, 1)]),
            send(cut, [(1, 3), (0, 2)]),
            send(cut, [(0, 3), (1, 2)]),
        ]
        mine = jnp.concatenate([along[m - 1] for m in places], axis=0)
        plane = [mine] + [swap(mine, "dp", m, groups) for m in (2, 4, 6)]
        later = lax.optimization_barrier((patches, mine))[0]
        patch_list = [
            patches,
            send(later, [(2, 3), (3, 2)]),
            send(patches, [(1, 3), (3, 1)]),
            send(patches, [(0, 3), (1, 2), (2, 1), (3, 0)]),
        ]
        slots = (0, 1, 2, 3)
        own_slots = (0, 2, 3)
        own_patches = [patch_list[i] for i in own_slots]
    else:
        slots = places = own_slots = None
        patch_list = own_patches = [lax.all_gather(patches, "seq", axis=0, tiled=True)]
        pos_list = [lax.all_gather(pos_embed, "seq", axis=0, tiled=False)]
    here = VMEM if quick else jax.ShapeDtypeStruct
    state = (here((H, rows, head + LANES), F32), here((H, rows, LANES), F32))
    held = VMEM((count * rows + PAD, feats), BF16)
    n = len(own_patches)
    hidden, query, acc, top, flipped = pl.pallas_call(
        functools.partial(own_kernel, own_slots, count, n),
        out_shape=(here((rows, width), F32), here((rows, width), BF16), *state, here((rows, feats), F32)),
        in_specs=spec(n + 7),
        out_specs=spec(5),
        scratch_shapes=[held],
        compiler_params=pltpu.CompilerParams(vmem_limit_bytes=(16 if quick else 48) << 20),
        cost_estimate=cost(1 << 36),
        name="own_block",
    )(*own_patches, w_in, b_in, pos_embed, ln_gain, w_query, w_key, w_value)
    n = len(patch_list)
    if quick:
        patch_list[1], query = lax.optimization_barrier((patch_list[1], query))
        near = swap(mine, "dp", 1, groups)
        near, b_in = lax.optimization_barrier((near, b_in))
    parts = pl.pallas_call(
        functools.partial(parts_kernel, slots, places, count, n),
        out_shape=here((count - 1, rows, width), F32),
        in_specs=spec(n + 2),
        out_specs=spec(1)[0],
        scratch_shapes=[held],
        compiler_params=pltpu.CompilerParams(vmem_limit_bytes=(10 if quick else 48) << 20),
        cost_estimate=cost(1 << 30),
        name="patch_parts",
    )(*patch_list, w_in, b_in)
    if quick:
        parts, *plane = lax.optimization_barrier((parts, *plane))
        plane = jnp.stack(plane[1:])
        pos_list = (mine, near, plane, swap(plane, "dp", 1, groups))
    n = len(pos_list)
    latent, logdet, _, _ = pl.pallas_call(
        functools.partial(rest_kernel, places, n),
        out_shape=(jax.ShapeDtypeStruct((rows, feats), F32), jax.ShapeDtypeStruct((rows,), F32)) + state,
        in_specs=spec(n + 13),
        out_specs=spec(4),
        scratch_shapes=[VMEM((groups, (count - 1) * rows, LANES), BF16)] + [VMEM(((count - 1) * rows, width), BF16)] * 3
        if quick
        else [],
        input_output_aliases={2: 2, 3: 3},
        compiler_params=pltpu.CompilerParams(vmem_limit_bytes=(20 if quick else 60) << 20),
        cost_estimate=cost(1),
        name="other_blocks",
    )(hidden, query, acc, top, parts, flipped, *pos_list, ln_gain, w_key, w_value, w_proj, out_gain, w_out, b_out)
    return (latent, logdet)


def solution(mesh):
    in_specs = (
        P(("dp", "seq"), None),
        P("seq", None),
        P(),
        P(),
        P(),
        P(),
        P(),
        P(),
        P(),
        P(),
        P(),
        P(),
    )
    out_specs = (P(("dp", "seq"), None), P(("dp", "seq")))
    return jax.shard_map(shards, mesh=mesh, in_specs=in_specs, out_specs=out_specs, check_vma=False)
```
